32 devices in a mesh: groups: 2 (over x), tm: 16 (over z, y, core).
Axes of the slice: x: 2, y: 2, z: 4, core: 2. Of those that a mesh axis runs over, the one named last changes fastest.
Arguments:
- inputs: bfloat16 [32768, 1536], P(('groups', 'tm')), parts along dimension 0
- counts: int32 [32], P(('groups', 'tm')), parts along dimension 0, may hold values from 1 to 1024, as said below
- query_weight: bfloat16 [1536, 1024], replicated
- key_weight: bfloat16 [1536, 1024], replicated
- value_weight: bfloat16 [1536, 1024], replicated, may hold values from -0.625 to 0.625
Outputs:
- attended: bfloat16 [32768, 1024], P(('groups', 'tm')), parts along dimension 0
The draws below stay inside these ranges and needn't reach their ends.
There are 2 independent parts, one for each index of `groups`. The reference program is written for one: setup_inputs(seed, part) draws one part's arguments, and reference() takes and returns one part's arrays. A program takes and returns all parts, laid end to end along the dimension named above; an argument that names none is the same for every part. Nothing has to cross between parts.
Inputs may be any that keep to these rules, and one draw needn't show every extreme that they name: `counts`: each entry is the number of valid frames at the start of that index's 1024 frames; at least one entry equals 1024.
All inputs are finite; a program needn't handle non-finite values.
Results may differ from the reference program's by a relative error of at most 0.0085.
Values may be sent and summed in bfloat16 or wider, within the bound.
A program may use at most 192 MiB of HBM per device.

```python
import jax
import jax.numpy as jnp
from jax import lax

D = 1536
HEADS = 16
DH = 64
WINDOW = 128
L = 1024
FRAMES = 16384


def weight_pair(key):
    shape = (D, HEADS * DH)
    base = jax.random.normal(jax.random.fold_in(key, 11), shape, jnp.float32) * D ** (-0.5)
    noise = jax.random.normal(jax.random.fold_in(key, 12), shape, jnp.float32) * D ** (-0.5)
    return (base, noise)


def draw_query_weight(key, part):
    base, noise = weight_pair(key)
    return base.astype(jnp.bfloat16)


def draw_key_weight(key, part):
    base, noise = weight_pair(key)
    return noise.astype(jnp.bfloat16)


def draw_inputs(key, part):
    values = jax.random.normal(jax.random.fold_in(key, 21), (FRAMES, D), jnp.float32)
    return jnp.clip(values, -6.0, 6.0).astype(jnp.bfloat16)


def draw_counts(key, part):
    shards = FRAMES // L
    partial_counts = jax.random.randint(jax.random.fold_in(key, 31), (shards,), 1, L + 1)
    full_flags = jax.random.randint(jax.random.fold_in(key, 32), (shards,), 0, 2)
    result = jnp.where(full_flags == 1, L, partial_counts)
    picked = jax.random.randint(jax.random.fold_in(key, 33), (), 0, shards)
    return result.at[picked].set(L).astype(jnp.int32)


def gaussian(own_key, extent, scale, reach, kind=jnp.bfloat16):
    values = scale * jax.random.normal(own_key, extent, jnp.float32)
    return jnp.clip(values, min=-reach, max=reach).astype(kind)


def setup_inputs(seed: int = 0, part: int = 0) -> dict:
    arg_keys = jax.random.split(jax.random.key(seed), 6)
    own_keys = jax.random.split(jax.random.fold_in(arg_keys[5], part), 6)
    return {
        "inputs": draw_inputs(jax.random.fold_in(jax.random.fold_in(arg_keys[5], part), 71), part),
        "counts": draw_counts(jax.random.fold_in(jax.random.fold_in(arg_keys[5], part), 71), part),
        "query_weight": draw_query_weight(jax.random.fold_in(arg_keys[5], 71), part),
        "key_weight": draw_key_weight(jax.random.fold_in(arg_keys[5], 71), part),
        "value_weight": gaussian(arg_keys[4], (D, HEADS * DH), (D // 16) ** -0.5, 0.625),
    }


def normalize(rows):
    values = rows.astype(jnp.float32)
    average = lax.optimization_barrier(jnp.mean(values, axis=-1, keepdims=True))
    centred = values - average
    spread = lax.optimization_barrier(jnp.mean(centred * centred, axis=-1, keepdims=True))
    return (centred * lax.rsqrt(spread + 1e-05)).astype(jnp.bfloat16)

def attend(queries, key_rows, value_rows, key_valid, query_valid):
    rows = queries.shape[0]
    span = key_rows.shape[0]
    width = (span - rows) // 2
    heads = queries.shape[1] // DH
    q_heads = queries.reshape(rows, heads, DH).astype(jnp.float32)
    k_heads = key_rows.reshape(span, heads, DH).astype(jnp.float32)
    v_heads = value_rows.reshape(span, heads, DH).astype(jnp.float32)
    scores = jnp.einsum('qhd,khd->hqk', q_heads, k_heads) * DH ** (-0.5)
    offset = jnp.arange(span, dtype=jnp.int32)[None, :] - width - jnp.arange(rows, dtype=jnp.int32)[:, None]
    allowed = (jnp.abs(offset) <= width) & (key_valid[None, :] | (offset == 0))
    peak = lax.optimization_barrier(jnp.max(jnp.where(allowed, scores, -jnp.inf), axis=-1, keepdims=True))
    expo = jnp.where(allowed, jnp.exp(scores - peak), 0.0)
    probs = (expo / lax.optimization_barrier(jnp.sum(expo, axis=-1, keepdims=True))).astype(jnp.bfloat16)
    mixed = jnp.einsum('hqk,khd->qhd', probs.astype(jnp.float32), v_heads).reshape(rows, heads * DH)
    return jnp.where(query_valid[:, None], mixed, 0.0).astype(jnp.bfloat16)

def reference(inputs, counts, query_weight, key_weight, value_weight):
    shards = FRAMES // L
    normed = normalize(inputs)
    queries = jnp.dot(normed, query_weight, preferred_element_type=jnp.float32).astype(jnp.bfloat16)
    keys = jnp.dot(normed, key_weight, preferred_element_type=jnp.float32).astype(jnp.bfloat16)
    values = jnp.dot(normed, value_weight, preferred_element_type=jnp.float32).astype(jnp.bfloat16)
    frame_ids = jnp.arange(FRAMES, dtype=jnp.int32)
    frame_valid = frame_ids % L < counts[frame_ids // L]
    keys_padded = jnp.pad(keys, ((WINDOW, WINDOW), (0, 0)))
    values_padded = jnp.pad(values, ((WINDOW, WINDOW), (0, 0)))
    valid_padded = jnp.pad(frame_valid, (WINDOW, WINDOW))
    width_all = queries.shape[1]

    def one_shard(index):
        start = (index * L).astype(jnp.int32)
        zero = jnp.zeros((), jnp.int32)
        block_q = lax.dynamic_slice(queries, (start, zero), (L, width_all))
        block_k = lax.dynamic_slice(keys_padded, (start, zero), (L + 2 * WINDOW, width_all))
        block_v = lax.dynamic_slice(values_padded, (start, zero), (L + 2 * WINDOW, width_all))
        block_valid = lax.dynamic_slice(valid_padded, (start,), (L + 2 * WINDOW,))
        query_valid = jnp.arange(L, dtype=jnp.int32) < counts[index]
        return attend(block_q, block_k, block_v, block_valid, query_valid)
    blocks = lax.map(one_shard, jnp.arange(shards, dtype=jnp.int32))
    return blocks.reshape(FRAMES, width_all)
```

```python
import functools

import jax
import jax.numpy as jnp
from jax import lax
from jax.experimental import pallas as pl
from jax.experimental.pallas import tpu as pltpu
from jax.sharding import PartitionSpec as P

DH = 64
WINDOW = 128
PAIR = 2 * DH
SPAN = 3 * WINDOW
LOG2E = 1.4426950408889634
MESH = pl.DeviceIdType.MESH
NT = (((1,), (1,)), ((), ()))


def normalize(rows):
    values = rows.astype(jnp.float32)
    average = jnp.mean(values, axis=-1, keepdims=True)
    centred = values - average
    spread = jnp.mean(centred * centred, axis=-1, keepdims=True)
    return (centred * lax.rsqrt(spread + 1e-05)).astype(jnp.bfloat16)


def kernel(
    counts, x_hbm, wq_hbm, wk_hbm, wv_hbm, out_hbm,
    x, wq, wk, wv, q, k, v, o, bias, cnt, cnt_near,
    x_sem, w_sem, out_sem, send_sem, recv_sem,
):
    rows, width = out_hbm.shape
    blocks = rows // WINDOW
    tm = lax.axis_size("tm")
    me = lax.axis_index("tm")
    has_left, has_right = me > 0, me < tm - 1
    barrier = pltpu.get_barrier_semaphore()

    @pl.when(has_left)
    def _():
        pl.semaphore_signal(barrier, inc=1, device_id={"tm": me - 1}, device_id_type=MESH)

    @pl.when(has_right)
    def _():
        pl.semaphore_signal(barrier, inc=1, device_id={"tm": me + 1}, device_id_type=MESH)

    chunk = 256
    x_copy = [
        pltpu.make_async_copy(
            x_hbm.at[pl.ds(c * chunk, chunk)], x.at[pl.ds(c * chunk, chunk)], x_sem.at[c]
        )
        for c in range(rows // chunk)
    ]
    w_copy = [
        pltpu.make_async_copy(src, dst, w_sem.at[n])
        for n, (src, dst) in enumerate(((wk_hbm, wk), (wv_hbm, wv), (wq_hbm, wq)))
    ]
    for copy in x_copy + w_copy:
        copy.start()
    cnt[...] = jnp.full(cnt.shape, counts[0], jnp.int32)

    def remote(n, src, dst, to):
        return pltpu.make_async_remote_copy(
            src_ref=src, dst_ref=dst, send_sem=send_sem.at[n], recv_sem=recv_sem.at[n],
            device_id={"tm": to}, device_id_type=MESH,
        )

    first, last = pl.ds(WINDOW, WINDOW), pl.ds(rows, WINDOW)
    before, after = pl.ds(0, WINDOW), pl.ds(rows + WINDOW, WINDOW)
    to_right = [
        remote(0, cnt, cnt_near.at[0], me + 1),
        remote(1, k.at[last], k.at[before], me + 1),
        remote(2, v.at[last], v.at[before], me + 1),
    ]
    to_left = [
        remote(3, cnt, cnt_near.at[1], me - 1),
        remote(4, k.at[first], k.at[after], me - 1),
        remote(5, v.at[first], v.at[after], me - 1),
    ]

    def send(n):
        @pl.when(has_right)
        def _():
            to_right[n].start()

        @pl.when(has_left)
        def _():
            to_left[n].start()

    for c in range(rows // chunk):
        x_copy[c].wait()

        def norm(t, carry, c=c):
            part = pl.ds(pl.multiple_of(c * chunk + t * 64, 64), 64)
            x[part] = normalize(x[part])
            return carry

        lax.fori_loop(0, chunk // 64, norm, 0)

    def project(w, dst, shift, scale):
        def step(t, carry):
            col = pl.ds(pl.multiple_of((t // 2) * 256, 256), 256)
            at = (t % 2) * (rows // 2)
            src = pl.ds(pl.multiple_of(at, 256), rows // 2)
            to = pl.ds(pl.multiple_of(at + shift, 128), rows // 2)
            y = jnp.dot(x[src], w[:, col], preferred_element_type=jnp.float32)
            if scale != 1.0:
                y = y * scale
            dst[to, col] = y.astype(jnp.bfloat16)
            return carry

        lax.fori_loop(0, 2 * (width // 256), step, 0)

    w_copy[0].wait()
    project(wk, k, WINDOW, 1.0)

    pl.semaphore_wait(barrier, has_left.astype(jnp.int32) + has_right.astype(jnp.int32))
    send(0)
    send(1)
    w_copy[1].wait()
    project(wv, v, WINDOW, 1.0)
    send(2)
    w_copy[2].wait()
    project(wq, q, 0, DH ** (-0.5) * LOG2E)

    row = lax.broadcasted_iota(jnp.int32, (WINDOW, SPAN), 0)
    lane = lax.broadcasted_iota(jnp.int32, (WINDOW, SPAN), 1)
    offset = lane - WINDOW - row
    head_a = lax.broadcasted_iota(jnp.int32, (WINDOW, PAIR), 1) < DH
    row_id = lax.broadcasted_iota(jnp.int32, (WINDOW, PAIR), 0)
    ones = jnp.ones((SPAN, PAIR), jnp.bfloat16)

    def set_bias(valid):
        allowed = (jnp.abs(offset) <= WINDOW) & (valid | (offset == 0))
        bias[...] = jnp.where(allowed, 0.0, -jnp.inf)

    def block(t, carry):
        b = (t + 1) % blocks
        r = pl.multiple_of(b * WINDOW, WINDOW)
        place = lane + (r - WINDOW)

        @pl.when(t < blocks - 2)
        def _():
            set_bias(place < counts[0])

        @pl.when(t == blocks - 2)
        def _():
            @pl.when(has_right)
            def _():
                for copy in to_left:
                    copy.wait_recv()

            @pl.when(jnp.logical_not(has_right))
            def _():
                cnt_near[1] = jnp.zeros(cnt.shape, jnp.int32)
                k[after] = jnp.zeros((WINDOW, width), jnp.bfloat16)
                v[after] = jnp.zeros((WINDOW, width), jnp.bfloat16)

            near = jnp.concatenate([cnt_near[1, 0:1, :]] * 3, axis=1)
            limit = jnp.where(lane[0:1] < 2 * WINDOW, counts[0], near + rows)
            set_bias(place < limit)

        @pl.when(t == blocks - 1)
        def _():
            @pl.when(has_left)
            def _():
                for copy in to_right:
                    copy.wait_recv()

            @pl.when(jnp.logical_not(has_left))
            def _():
                cnt_near[0] = jnp.zeros(cnt.shape, jnp.int32)
                k[before] = jnp.zeros((WINDOW, width), jnp.bfloat16)
                v[before] = jnp.zeros((WINDOW, width), jnp.bfloat16)

            near = jnp.concatenate([cnt_near[0, 0:1, :]] * 3, axis=1)
            limit = jnp.where(lane[0:1] < WINDOW, near - rows, counts[0])
            set_bias(place < limit)

        kept = row_id + r < counts[0]
        for p in range(width // PAIR):
            cols = slice(p * PAIR, (p + 1) * PAIR)
            q_pair = q[pl.ds(r, WINDOW), cols]
            zero = jnp.zeros_like(q_pair)
            stacked = jnp.concatenate(
                [jnp.where(head_a, q_pair, zero), jnp.where(head_a, zero, q_pair)], axis=0
            )
            s = lax.dot_general(
                stacked, k[pl.ds(r, SPAN), cols], NT, preferred_element_type=jnp.float32
            )
            s = s + jnp.concatenate([bias[...], bias[...]], axis=0)
            e = jnp.exp2(s - jnp.max(s, axis=-1, keepdims=True)).astype(jnp.bfloat16)
            wide = jnp.concatenate([v[pl.ds(r, SPAN), cols], ones], axis=1)
            m = jnp.dot(e, wide, preferred_element_type=jnp.float32)
            mixed = jnp.where(head_a, m[:WINDOW, :PAIR], m[WINDOW:, :PAIR])
            total = jnp.where(head_a, m[:WINDOW, PAIR:], m[WINDOW:, PAIR:])
            o[pl.ds(r, WINDOW), cols] = jnp.where(kept, mixed / total, 0.0).astype(jnp.bfloat16)
        pltpu.make_async_copy(
            o.at[pl.ds(r, WINDOW)], out_hbm.at[pl.ds(r, WINDOW)], out_sem.at[b]
        ).start()
        return carry

    lax.fori_loop(0, blocks, block, 0)

    for b in range(blocks):
        part = pl.ds(b * WINDOW, WINDOW)
        pltpu.make_async_copy(o.at[part], out_hbm.at[part], out_sem.at[b]).wait()

    @pl.when(has_right)
    def _():
        for copy in to_right:
            copy.wait_send()

    @pl.when(has_left)
    def _():
        for copy in to_left:
            copy.wait_send()


def local(inputs, counts, query_weight, key_weight, value_weight):
    rows, depth = inputs.shape
    width = query_weight.shape[1]
    bf16 = jnp.bfloat16
    anywhere = pl.BlockSpec(memory_space=pl.ANY)
    macs = rows * width * (3 * depth + 4 * SPAN)
    return pl.pallas_call(
        kernel,
        out_shape=jax.ShapeDtypeStruct((rows, width), bf16),
        in_specs=[pl.BlockSpec(memory_space=pltpu.SMEM)] + [anywhere] * 4,
        out_specs=anywhere,
        scratch_shapes=[
            pltpu.VMEM((rows, depth), bf16),
            pltpu.VMEM((depth, width), bf16),
            pltpu.VMEM((depth, width), bf16),
            pltpu.VMEM((depth, width), bf16),
            pltpu.VMEM((rows, width), bf16),
            pltpu.VMEM((rows + 2 * WINDOW, width), bf16),
            pltpu.VMEM((rows + 2 * WINDOW, width), bf16),
            pltpu.VMEM((rows, width), bf16),
            pltpu.VMEM((WINDOW, SPAN), jnp.float32),
            pltpu.VMEM((8, 128), jnp.int32),
            pltpu.VMEM((2, 8, 128), jnp.int32),
            pltpu.SemaphoreType.DMA((rows // 256,)),
            pltpu.SemaphoreType.DMA((3,)),
            pltpu.SemaphoreType.DMA((rows // WINDOW,)),
            pltpu.SemaphoreType.DMA((6,)),
            pltpu.SemaphoreType.DMA((6,)),
        ],
        compiler_params=pltpu.CompilerParams(
            collective_id=0, has_side_effects=True, vmem_limit_bytes=48 * 1024 * 1024
        ),
        cost_estimate=pl.CostEstimate(
            flops=2 * macs, bytes_accessed=15 * 2**20, transcendentals=rows * SPAN * width // DH
        ),
    )(counts, inputs, query_weight, key_weight, value_weight)


def solution(mesh):
    placed = (P(("groups", "tm"), None), P(("groups", "tm")), P(), P(), P())
    return jax.shard_map(
        local, mesh=mesh, in_specs=placed, out_specs=P(("groups", "tm"), None), check_vma=False
    )
```

```python
import functools

import jax
import jax.numpy as jnp
from jax import lax
from jax.experimental import pallas as pl
from jax.experimental.pallas import tpu as pltpu
from jax.sharding import PartitionSpec as P

DH = 64
WINDOW = 128
PAIR = 2 * DH
SPAN = 3 * WINDOW
LOG2E = 1.4426950408889634
MESH = pl.DeviceIdType.MESH
NT = (((1,), (1,)), ((), ()))


def normalize(rows):
    values = rows.astype(jnp.float32)
    average = jnp.mean(values, axis=-1, keepdims=True)
    centred = values - average
    spread = jnp.mean(centred * centred, axis=-1, keepdims=True)
    return (centred * lax.rsqrt(spread + 1e-05)).astype(jnp.bfloat16)


def kernel(
    counts, x_hbm, wq_hbm, wk_hbm, wv_hbm, out_hbm,
    x, wq, wk, wv, q, k, v, o, bias, sb, mb, cnt, cnt_near,
    x_sem, w_sem, out_sem, send_sem, recv_sem,
):
    rows, width = out_hbm.shape
    blocks = rows // WINDOW
    tm = lax.axis_size("tm")
    me = lax.axis_index("tm")
    has_left, has_right = me > 0, me < tm - 1
    barrier = pltpu.get_barrier_semaphore()

    @pl.when(has_left)
    def _():
        pl.semaphore_signal(barrier, inc=1, device_id={"tm": me - 1}, device_id_type=MESH)

    @pl.when(has_right)
    def _():
        pl.semaphore_signal(barrier, inc=1, device_id={"tm": me + 1}, device_id_type=MESH)

    chunk = 256
    x_copy = [
        pltpu.make_async_copy(
            x_hbm.at[pl.ds(c * chunk, chunk)], x.at[pl.ds(c * chunk, chunk)], x_sem.at[c]
        )
        for c in range(rows // chunk)
    ]
    w_copy = [
        pltpu.make_async_copy(src, dst, w_sem.at[n])
        for n, (src, dst) in enumerate(((wk_hbm, wk), (wv_hbm, wv), (wq_hbm, wq)))
    ]
    for copy in x_copy + w_copy:
        copy.start()
    cnt[...] = jnp.full(cnt.shape, counts[0], jnp.int32)

    def remote(n, src, dst, to):
        return pltpu.make_async_remote_copy(
            src_ref=src, dst_ref=dst, send_sem=send_sem.at[n], recv_sem=recv_sem.at[n],
            device_id={"tm": to}, device_id_type=MESH,
        )

    first, last = pl.ds(WINDOW, WINDOW), pl.ds(rows, WINDOW)
    before, after = pl.ds(0, WINDOW), pl.ds(rows + WINDOW, WINDOW)
    to_right = [
        remote(0, cnt, cnt_near.at[0], me + 1),
        remote(1, k.at[last], k.at[before], me + 1),
        remote(2, v.at[last], v.at[before], me + 1),
    ]
    to_left = [
        remote(3, cnt, cnt_near.at[1], me - 1),
        remote(4, k.at[first], k.at[after], me - 1),
        remote(5, v.at[first], v.at[after], me - 1),
    ]

    def send(n):
        @pl.when(has_right)
        def _():
            to_right[n].start()

        @pl.when(has_left)
        def _():
            to_left[n].start()

    for c in range(rows // chunk):
        x_copy[c].wait()

        def norm(t, carry, c=c):
            part = pl.ds(pl.multiple_of(c * chunk + t * 32, 32), 32)
            x[part] = normalize(x[part])
            return carry

        lax.fori_loop(0, chunk // 32, norm, 0, unroll=True)

    def project(w, dst, shift, scale):
        def step(t, carry):
            col = pl.ds(pl.multiple_of((t // 2) * 256, 256), 256)
            at = (t % 2) * (rows // 2)
            src = pl.ds(pl.multiple_of(at, 256), rows // 2)
            to = pl.ds(pl.multiple_of(at + shift, 128), rows // 2)
            y = jnp.dot(x[src], w[:, col], preferred_element_type=jnp.float32)
            if scale != 1.0:
                y = y * scale
            dst[to, col] = y.astype(jnp.bfloat16)
            return carry

        lax.fori_loop(0, 2 * (width // 256), step, 0, unroll=True)

    w_copy[0].wait()
    project(wk, k, WINDOW, 1.0)

    pl.semaphore_wait(barrier, has_left.astype(jnp.int32) + has_right.astype(jnp.int32))
    send(0)
    send(1)
    w_copy[1].wait()
    project(wv, v, WINDOW, 1.0)
    send(2)
    w_copy[2].wait()
    project(wq, q, 0, DH ** (-0.5) * LOG2E)

    row = lax.broadcasted_iota(jnp.int32, (WINDOW, SPAN), 0)
    lane = lax.broadcasted_iota(jnp.int32, (WINDOW, SPAN), 1)
    offset = lane - WINDOW - row
    head_a = lax.broadcasted_iota(jnp.int32, (WINDOW, PAIR), 1) < DH
    row_id = lax.broadcasted_iota(jnp.int32, (WINDOW, PAIR), 0)
    ones = jnp.ones((SPAN, PAIR), jnp.bfloat16)

    def set_bias(valid):
        allowed = (jnp.abs(offset) <= WINDOW) & (valid | (offset == 0))
        bias[...] = jnp.where(allowed, 0.0, -jnp.inf)

    def block(t, carry):
        b = (t + 1) % blocks
        r = pl.multiple_of(b * WINDOW, WINDOW)
        place = lane + (r - WINDOW)

        @pl.when(t < blocks - 2)
        def _():
            set_bias(place < counts[0])

        @pl.when(t == blocks - 2)
        def _():
            @pl.when(has_right)
            def _():
                for copy in to_left:
                    copy.wait_recv()

            @pl.when(jnp.logical_not(has_right))
            def _():
                cnt_near[1] = jnp.zeros(cnt.shape, jnp.int32)
                k[after] = jnp.zeros((WINDOW, width), jnp.bfloat16)
                v[after] = jnp.zeros((WINDOW, width), jnp.bfloat16)

            near = jnp.concatenate([cnt_near[1, 0:1, :]] * 3, axis=1)
            limit = jnp.where(lane[0:1] < 2 * WINDOW, counts[0], near + rows)
            set_bias(place < limit)

        @pl.when(t == blocks - 1)
        def _():
            @pl.when(has_left)
            def _():
                for copy in to_right:
                    copy.wait_recv()

            @pl.when(jnp.logical_not(has_left))
            def _():
                cnt_near[0] = jnp.zeros(cnt.shape, jnp.int32)
                k[before] = jnp.zeros((WINDOW, width), jnp.bfloat16)
                v[before] = jnp.zeros((WINDOW, width), jnp.bfloat16)

            near = jnp.concatenate([cnt_near[0, 0:1, :]] * 3, axis=1)
            limit = jnp.where(lane[0:1] < WINDOW, near - rows, counts[0])
            set_bias(place < limit)

        kept = row_id + r < counts[0]
        def scores(p):
            cols = slice(p * PAIR, (p + 1) * PAIR)
            q_pair = q[pl.ds(r, WINDOW), cols]
            zero = jnp.zeros_like(q_pair)
            stacked = jnp.concatenate(
                [jnp.where(head_a, q_pair, zero), jnp.where(head_a, zero, q_pair)], axis=0
            )
            s = lax.dot_general(
                stacked, k[pl.ds(r, SPAN), cols], NT, preferred_element_type=jnp.float32
            )
            return s + jnp.concatenate([bias[...], bias[...]], axis=0)

        def mix(p, e):
            cols = slice(p * PAIR, (p + 1) * PAIR)
            wide = jnp.concatenate([v[pl.ds(r, SPAN), cols], ones], axis=1)
            m = jnp.dot(e, wide, preferred_element_type=jnp.float32)
            mixed = jnp.where(head_a, m[:WINDOW, :PAIR], m[WINDOW:, :PAIR])
            total = jnp.where(head_a, m[:WINDOW, PAIR:], m[WINDOW:, PAIR:])
            o[pl.ds(r, WINDOW), cols] = jnp.where(kept, mixed / total, 0.0).astype(jnp.bfloat16)

        pairs = width // PAIR
        for p in range(pairs):
            s = scores(p)
            sb[p] = s
            mb[p] = jnp.broadcast_to(jnp.max(s, axis=-1, keepdims=True), (2 * WINDOW, PAIR))
        for p in range(pairs):
            top = jnp.concatenate([mb[p]] * 3, axis=1)
            mix(p, jnp.exp2(sb[p] - top).astype(jnp.bfloat16))
        pltpu.make_async_copy(
            o.at[pl.ds(r, WINDOW)], out_hbm.at[pl.ds(r, WINDOW)], out_sem.at[b]
        ).start()
        return carry

    lax.fori_loop(0, blocks, block, 0)

    for b in range(blocks):
        part = pl.ds(b * WINDOW, WINDOW)
        pltpu.make_async_copy(o.at[part], out_hbm.at[part], out_sem.at[b]).wait()

    @pl.when(has_right)
    def _():
        for copy in to_right:
            copy.wait_send()

    @pl.when(has_left)
    def _():
        for copy in to_left:
            copy.wait_send()


def local(inputs, counts, query_weight, key_weight, value_weight):
    rows, depth = inputs.shape
    width = query_weight.shape[1]
    bf16 = jnp.bfloat16
    anywhere = pl.BlockSpec(memory_space=pl.ANY)
    macs = rows * width * (3 * depth + 4 * SPAN)
    return pl.pallas_call(
        kernel,
        out_shape=jax.ShapeDtypeStruct((rows, width), bf16),
        in_specs=[pl.BlockSpec(memory_space=pltpu.SMEM)] + [anywhere] * 4,
        out_specs=anywhere,
        scratch_shapes=[
            pltpu.VMEM((rows, depth), bf16),
            pltpu.VMEM((depth, width), bf16),
            pltpu.VMEM((depth, width), bf16),
            pltpu.VMEM((depth, width), bf16),
            pltpu.VMEM((rows, width), bf16),
            pltpu.VMEM((rows + 2 * WINDOW, width), bf16),
            pltpu.VMEM((rows + 2 * WINDOW, width), bf16),
            pltpu.VMEM((rows, width), bf16),
            pltpu.VMEM((WINDOW, SPAN), jnp.float32),
            pltpu.VMEM((width // PAIR, 2 * WINDOW, SPAN), jnp.float32),
            pltpu.VMEM((width // PAIR, 2 * WINDOW, PAIR), jnp.float32),
            pltpu.VMEM((8, 128), jnp.int32),
            pltpu.VMEM((2, 8, 128), jnp.int32),
            pltpu.SemaphoreType.DMA((rows // 256,)),
            pltpu.SemaphoreType.DMA((3,)),
            pltpu.SemaphoreType.DMA((rows // WINDOW,)),
            pltpu.SemaphoreType.DMA((6,)),
            pltpu.SemaphoreType.DMA((6,)),
        ],
        compiler_params=pltpu.CompilerParams(
            collective_id=0, has_side_effects=True, vmem_limit_bytes=50 * 1024 * 1024
        ),
        cost_estimate=pl.CostEstimate(
            flops=2 * macs, bytes_accessed=15 * 2**20, transcendentals=rows * SPAN * width // DH
        ),
    )(counts, inputs, query_weight, key_weight, value_weight)


def solution(mesh):
    placed = (P(("groups", "tm"), None), P(("groups", "tm")), P(), P(), P())
    return jax.shard_map(
        local, mesh=mesh, in_specs=placed, out_specs=P(("groups", "tm"), None), check_vma=False
    )
```

```python
import functools

import jax
import jax.numpy as jnp
from jax import lax
from jax.experimental import pallas as pl
from jax.experimental.pallas import tpu as pltpu
from jax.sharding import PartitionSpec as P

DH = 64
WINDOW = 128
PAIR = 2 * DH
SPAN = 3 * WINDOW
LOG2E = 1.4426950408889634
MESH = pl.DeviceIdType.MESH
NT = (((1,), (1,)), ((), ()))


def normalize(rows):
    values = rows.astype(jnp.float32)
    average = jnp.mean(values, axis=-1, keepdims=True)
    centred = values - average
    spread = jnp.mean(centred * centred, axis=-1, keepdims=True)
    return (centred * lax.rsqrt(spread + 1e-05)).astype(jnp.bfloat16)


def kernel(
    counts, x_hbm, wq_hbm, wk_hbm, wv_hbm, out_hbm,
    x, wq, wk, wv, q, k, v, o, bias, sb, mb, cnt, cnt_near,
    x_sem, w_sem, out_sem, send_sem, recv_sem,
):
    rows, width = out_hbm.shape
    blocks = rows // WINDOW
    tm = lax.axis_size("tm")
    me = lax.axis_index("tm")
    has_left, has_right = me > 0, me < tm - 1
    barrier = pltpu.get_barrier_semaphore()

    @pl.when(has_left)
    def _():
        pl.semaphore_signal(barrier, inc=1, device_id={"tm": me - 1}, device_id_type=MESH)

    @pl.when(has_right)
    def _():
        pl.semaphore_signal(barrier, inc=1, device_id={"tm": me + 1}, device_id_type=MESH)

    chunk = 256
    x_copy = [
        pltpu.make_async_copy(
            x_hbm.at[pl.ds(c * chunk, chunk)], x.at[pl.ds(c * chunk, chunk)], x_sem.at[c]
        )
        for c in range(rows // chunk)
    ]
    w_copy = [
        pltpu.make_async_copy(src, dst, w_sem.at[n])
        for n, (src, dst) in enumerate(((wk_hbm, wk), (wv_hbm, wv), (wq_hbm, wq)))
    ]
    for copy in x_copy + w_copy:
        copy.start()
    cnt[...] = jnp.full(cnt.shape, counts[0], jnp.int32)

    def remote(n, src, dst, to):
        return pltpu.make_async_remote_copy(
            src_ref=src, dst_ref=dst, send_sem=send_sem.at[n], recv_sem=recv_sem.at[n],
            device_id={"tm": to}, device_id_type=MESH,
        )

    first, last = pl.ds(WINDOW, WINDOW), pl.ds(rows, WINDOW)
    before, after = pl.ds(0, WINDOW), pl.ds(rows + WINDOW, WINDOW)
    to_right = [
        remote(0, cnt, cnt_near.at[0], me + 1),
        remote(1, k.at[last], k.at[before], me + 1),
        remote(2, v.at[last], v.at[before], me + 1),
    ]
    to_left = [
        remote(3, cnt, cnt_near.at[1], me - 1),
        remote(4, k.at[first], k.at[after], me - 1),
        remote(5, v.at[first], v.at[after], me - 1),
    ]

    def send(n):
        @pl.when(has_right)
        def _():
            to_right[n].start()

        @pl.when(has_left)
        def _():
            to_left[n].start()

    for c in range(rows // chunk):
        x_copy[c].wait()

        def norm(t, carry, c=c):
            part = pl.ds(pl.multiple_of(c * chunk + t * 32, 32), 32)
            x[part] = normalize(x[part])
            return carry

        lax.fori_loop(0, chunk // 32, norm, 0, unroll=True)

    def project(w, dst, shift, scale):
        def step(t, carry):
            col = pl.ds(pl.multiple_of((t // 2) * 256, 256), 256)
            at = (t % 2) * (rows // 2)
            src = pl.ds(pl.multiple_of(at, 256), rows // 2)
            to = pl.ds(pl.multiple_of(at + shift, 128), rows // 2)
            y = jnp.dot(x[src], w[:, col], preferred_element_type=jnp.float32)
            if scale != 1.0:
                y = y * scale
            dst[to, col] = y.astype(jnp.bfloat16)
            return carry

        lax.fori_loop(0, 2 * (width // 256), step, 0, unroll=True)

    w_copy[0].wait()
    project(wk, k, WINDOW, 1.0)

    pl.semaphore_wait(barrier, has_left.astype(jnp.int32) + has_right.astype(jnp.int32))
    send(0)
    send(1)
    w_copy[1].wait()
    project(wv, v, WINDOW, 1.0)
    send(2)
    w_copy[2].wait()
    project(wq, q, 0, DH ** (-0.5) * LOG2E)

    row = lax.broadcasted_iota(jnp.int32, (WINDOW, SPAN), 0)
    lane = lax.broadcasted_iota(jnp.int32, (WINDOW, SPAN), 1)
    offset = lane - WINDOW - row
    head_a = lax.broadcasted_iota(jnp.int32, (WINDOW, PAIR), 1) < DH
    row_id = lax.broadcasted_iota(jnp.int32, (WINDOW, PAIR), 0)
    ones = jnp.ones((SPAN, PAIR), jnp.bfloat16)

    def set_bias(valid):
        allowed = (jnp.abs(offset) <= WINDOW) & (valid | (offset == 0))
        bias[...] = jnp.where(allowed, 0.0, -jnp.inf)

    pairs = width // PAIR

    def rows_of(t):
        return pl.multiple_of(((t + 1) % blocks) * WINDOW, WINDOW)

    def prepare(t):
        r = rows_of(t)
        place = lane + (r - WINDOW)

        @pl.when(t < blocks - 2)
        def _():
            set_bias(place < counts[0])

        @pl.when(t == blocks - 2)
        def _():
            @pl.when(has_right)
            def _():
                for copy in to_left:
                    copy.wait_recv()

            @pl.when(jnp.logical_not(has_right))
            def _():
                cnt_near[1] = jnp.zeros(cnt.shape, jnp.int32)
                k[after] = jnp.zeros((WINDOW, width), jnp.bfloat16)
                v[after] = jnp.zeros((WINDOW, width), jnp.bfloat16)

            near = jnp.concatenate([cnt_near[1, 0:1, :]] * 3, axis=1)
            limit = jnp.where(lane[0:1] < 2 * WINDOW, counts[0], near + rows)
            set_bias(place < limit)

        @pl.when(t == blocks - 1)
        def _():
            @pl.when(has_left)
            def _():
                for copy in to_right:
                    copy.wait_recv()

            @pl.when(jnp.logical_not(has_left))
            def _():
                cnt_near[0] = jnp.zeros(cnt.shape, jnp.int32)
                k[before] = jnp.zeros((WINDOW, width), jnp.bfloat16)
                v[before] = jnp.zeros((WINDOW, width), jnp.bfloat16)

            near = jnp.concatenate([cnt_near[0, 0:1, :]] * 3, axis=1)
            limit = jnp.where(lane[0:1] < WINDOW, near - rows, counts[0])
            set_bias(place < limit)

    def scores(t, p):
        r = rows_of(t)
        cols = slice(p * PAIR, (p + 1) * PAIR)
        q_pair = q[pl.ds(r, WINDOW), cols]
        zero = jnp.zeros_like(q_pair)
        stacked = jnp.concatenate(
            [jnp.where(head_a, q_pair, zero), jnp.where(head_a, zero, q_pair)], axis=0
        )
        s = lax.dot_general(
            stacked, k[pl.ds(r, SPAN), cols], NT, preferred_element_type=jnp.float32
        )
        s = s + jnp.concatenate([bias[...], bias[...]], axis=0)
        sb[p] = s
        mb[p] = jnp.broadcast_to(jnp.max(s, axis=-1, keepdims=True), (2 * WINDOW, PAIR))

    def mix(t, p):
        r = rows_of(t)
        cols = slice(p * PAIR, (p + 1) * PAIR)
        top = jnp.concatenate([mb[p]] * 3, axis=1)
        e = jnp.exp2(sb[p] - top).astype(jnp.bfloat16)
        wide = jnp.concatenate([v[pl.ds(r, SPAN), cols], ones], axis=1)
        m = jnp.dot(e, wide, preferred_element_type=jnp.float32)
        mixed = jnp.where(head_a, m[:WINDOW, :PAIR], m[WINDOW:, :PAIR])
        total = jnp.where(head_a, m[:WINDOW, PAIR:], m[WINDOW:, PAIR:])
        kept = row_id + r < counts[0]
        o[pl.ds(r, WINDOW), cols] = jnp.where(kept, mixed / total, 0.0).astype(jnp.bfloat16)

    def ship(t):
        r = rows_of(t)
        pltpu.make_async_copy(
            o.at[pl.ds(r, WINDOW)], out_hbm.at[pl.ds(r, WINDOW)], out_sem.at[(t + 1) % blocks]
        ).start()

    def block(t, carry):
        prepare(t + 1)
        for p in range(pairs):
            mix(t, p)
            scores(t + 1, p)
        ship(t)
        return carry

    prepare(0)
    for p in range(pairs):
        scores(0, p)
    lax.fori_loop(0, blocks - 1, block, 0)
    for p in range(pairs):
        mix(blocks - 1, p)
    ship(blocks - 1)

    for b in range(blocks):
        part = pl.ds(b * WINDOW, WINDOW)
        pltpu.make_async_copy(o.at[part], out_hbm.at[part], out_sem.at[b]).wait()

    @pl.when(has_right)
    def _():
        for copy in to_right:
            copy.wait_send()

    @pl.when(has_left)
    def _():
        for copy in to_left:
            copy.wait_send()


def local(inputs, counts, query_weight, key_weight, value_weight):
    rows, depth = inputs.shape
    width = query_weight.shape[1]
    bf16 = jnp.bfloat16
    anywhere = pl.BlockSpec(memory_space=pl.ANY)
    macs = rows * width * (3 * depth + 4 * SPAN)
    return pl.pallas_call(
        kernel,
        out_shape=jax.ShapeDtypeStruct((rows, width), bf16),
        in_specs=[pl.BlockSpec(memory_space=pltpu.SMEM)] + [anywhere] * 4,
        out_specs=anywhere,
        scratch_shapes=[
            pltpu.VMEM((rows, depth), bf16),
            pltpu.VMEM((depth, width), bf16),
            pltpu.VMEM((depth, width), bf16),
            pltpu.VMEM((depth, width), bf16),
            pltpu.VMEM((rows, width), bf16),
            pltpu.VMEM((rows + 2 * WINDOW, width), bf16),
            pltpu.VMEM((rows + 2 * WINDOW, width), bf16),
            pltpu.VMEM((rows, width), bf16),
            pltpu.VMEM((WINDOW, SPAN), jnp.float32),
            pltpu.VMEM((width // PAIR, 2 * WINDOW, SPAN), jnp.float32),
            pltpu.VMEM((width // PAIR, 2 * WINDOW, PAIR), jnp.float32),
            pltpu.VMEM((8, 128), jnp.int32),
            pltpu.VMEM((2, 8, 128), jnp.int32),
            pltpu.SemaphoreType.DMA((rows // 256,)),
            pltpu.SemaphoreType.DMA((3,)),
            pltpu.SemaphoreType.DMA((rows // WINDOW,)),
            pltpu.SemaphoreType.DMA((6,)),
            pltpu.SemaphoreType.DMA((6,)),
        ],
        compiler_params=pltpu.CompilerParams(
            collective_id=0, has_side_effects=True, vmem_limit_bytes=50 * 1024 * 1024
        ),
        cost_estimate=pl.CostEstimate(
            flops=2 * macs, bytes_accessed=15 * 2**20, transcendentals=rows * SPAN * width // DH
        ),
    )(counts, inputs, query_weight, key_weight, value_weight)


def solution(mesh):
    placed = (P(("groups", "tm"), None), P(("groups", "tm")), P(), P(), P())
    return jax.shard_map(
        local, mesh=mesh, in_specs=placed, out_specs=P(("groups", "tm"), None), check_vma=False
    )
```
